32 devices in a mesh: groups: 2 (over y), chan: 8 (over z, x), tm: 2 (over core).
Axes of the slice: x: 2, y: 2, z: 4, core: 2. Of those that a mesh axis runs over, the one named last changes fastest.
Arguments:
- record: bfloat16 [8, 4096, 1000], P('tm', ('groups', 'chan')), parts along dimension 1
- flags: int32 [4096], P(('groups', 'chan')), parts along dimension 0, may hold values 0 or 1
- plan: int32 [4], replicated, may hold values from 1 to 7, as said below
Outputs:
- stacked: bfloat16 [4, 4, 4096, 256], P('tm', None, ('groups', 'chan')), parts along dimension 2
The draws below stay inside these ranges and needn't reach their ends.
There are 2 independent parts, one for each index of `groups`. The reference program is written for one: setup_inputs(seed, part) draws one part's arguments, and reference() takes and returns one part's arrays. A program takes and returns all parts, laid end to end along the dimension named above; an argument that names none is the same for every part. Nothing has to cross between parts.
Inputs may be any that keep to these rules, and one draw needn't show every extreme that they name: `plan`: 4 distinct offsets; one of them equals 7.
All inputs are finite; a program needn't handle non-finite values. No bound on the sum of `flags` on one device may be relied on, other than what follows from the above.
Results may differ from the reference program's by a relative error of at most 0.0082.
Values may be sent and summed in bfloat16 or wider, within the bound.
A program may use at most 64 MiB of HBM per device.

```python
import math
import jax
import jax.numpy as jnp
from jax import lax

CH_DEV = 256
SAMPLES = 1000
NFREQ = 32
FLO = 5
LAGS = 4
LAGSTEP = 3
ROUNDS = 4
CHANNELS = 2048
WINDOWS = 8
N_CHAN = 8


def draw_record(key, part):
    scale_key, noise_key = jax.random.split(key, 2)
    shape = (WINDOWS, CHANNELS, SAMPLES)
    scales = jnp.exp(jax.random.uniform(scale_key, (WINDOWS, CHANNELS, 1), jnp.float32) * math.log(10.0))
    values = scales * jax.random.normal(noise_key, shape, jnp.float32)
    return values.astype(jnp.bfloat16)


def draw_plan(key, part):
    first_key, second_key = jax.random.split(key)
    others = jax.random.permutation(first_key, N_CHAN - 2)[:ROUNDS - 1] + 1
    values = jnp.concatenate([others.astype(jnp.int32), jnp.full((1,), N_CHAN - 1, jnp.int32)])
    order = jax.random.permutation(second_key, ROUNDS)
    return values[order].astype(jnp.int32)


def with_ends(result, rng, smallest, largest):
    extent = result.shape
    index_at = [jax.random.randint(jax.random.fold_in(rng, axis), (), 0, extent[axis]) for axis in range(len(extent))]
    result = result.at[tuple(index_at)].set(smallest)
    longest = extent.index(max(extent))
    index_at[longest] = (index_at[longest] + 1) % extent[longest]
    return result.at[tuple(index_at)].set(largest)


def setup_inputs(seed: int = 0, part: int = 0) -> dict:
    key_of = jax.random.split(jax.random.key(seed), 4)
    part_keys = jax.random.split(jax.random.fold_in(key_of[3], part), 4)
    return {
        "record": draw_record(jax.random.fold_in(jax.random.fold_in(key_of[3], part), 71), part),
        "flags": with_ends((jax.random.randint(part_keys[1], (CHANNELS,), 0, 8) < 7).astype(jnp.int32), jax.random.fold_in(part_keys[1], 1), 0, 1),
        "plan": draw_plan(jax.random.fold_in(key_of[3], 71), part),
    }


TWO_PI = 2.0 * math.pi

def prepare_traces(trace, flags):
    values = trace.astype(jnp.float32)
    centred = values - lax.optimization_barrier(jnp.mean(values, axis=-1, keepdims=True))
    spread = jnp.sqrt(lax.optimization_barrier(jnp.mean(centred * centred, axis=-1, keepdims=True)) + 1e-05)
    return (centred / spread * flags.astype(jnp.float32)[:, None]).astype(jnp.bfloat16)

def make_basis():
    times = jnp.arange(SAMPLES, dtype=jnp.int32)
    bins = FLO + jnp.arange(NFREQ, dtype=jnp.int32)
    phase = bins[:, None] * times[None, :] % SAMPLES
    angle = phase.astype(jnp.float32) * (TWO_PI / SAMPLES)
    table = jnp.stack([jnp.cos(angle), -jnp.sin(angle)], axis=1)
    return table.reshape(2 * NFREQ, SAMPLES).astype(jnp.bfloat16)

def lag_angles(first_bin, count_bins, lag_start, count_lags):
    lag_ticks = (lag_start + jnp.arange(count_lags, dtype=jnp.int32) - LAGS // 2) * LAGSTEP
    bins = FLO + first_bin + jnp.arange(count_bins, dtype=jnp.int32)
    phase = bins[None, :] * lag_ticks[:, None] % SAMPLES
    return phase.astype(jnp.float32) * (TWO_PI / SAMPLES)

def rotate_spectra(spectra, angles):
    real_part = spectra[:, :, 0, :].astype(jnp.float32)[None]
    imag_part = spectra[:, :, 1, :].astype(jnp.float32)[None]
    cosine = jnp.cos(angles)[:, None, :, None]
    sine = jnp.sin(angles)[:, None, :, None]
    first = real_part * cosine + imag_part * sine
    second = imag_part * cosine - real_part * sine
    return jnp.stack([first, second], axis=3).astype(jnp.bfloat16)

def reference(record, flags, plan):
    basis = make_basis()
    inverse = 1.0 / math.sqrt(SAMPLES)

    def one_window(trace):
        scaled = prepare_traces(trace, flags)
        return (jnp.dot(basis, scaled.T, preferred_element_type=jnp.float32) * inverse).astype(jnp.bfloat16)
    spectra = lax.map(one_window, record).reshape(WINDOWS, NFREQ, 2, CHANNELS)
    angles = lag_angles(0, NFREQ, 0, LAGS)
    scale_out = 1.0 / math.sqrt(WINDOWS * NFREQ)

    def one_block(block):
        own = lax.dynamic_slice_in_dim(spectra, block * CH_DEV, CH_DEV, 3)
        turned = rotate_spectra(own, angles).astype(jnp.float32)
        results = []
        for round_index in range(ROUNDS):
            other = jnp.bitwise_xor(block, plan[round_index]).astype(jnp.int32)
            partner = lax.dynamic_slice_in_dim(spectra, other * CH_DEV, CH_DEV, 3).astype(jnp.float32)
            piece = jnp.einsum('lwfpa,wfpb->lab', turned, partner) * scale_out
            results.append(piece.astype(jnp.bfloat16))
        return jnp.stack(results, axis=1)
    blocks = lax.map(one_block, jnp.arange(N_CHAN, dtype=jnp.int32))
    return blocks.transpose(1, 2, 0, 3, 4).reshape(LAGS, ROUNDS, CHANNELS, CH_DEV)
```

```python
from functools import partial
import math

import jax
import jax.numpy as jnp
import numpy as np
from jax import lax
from jax.experimental import pallas as pl
from jax.experimental.pallas import tpu as pltpu
from jax.sharding import PartitionSpec as P

SAMPLES = 1000
NFREQ = 32
FLO = 5
LAGS = 4
LAGSTEP = 3


TWO_PI = 2.0 * math.pi


def swapped(value, axis, apart):
    mask = 2**apart
    pairs = [(source, source ^ mask) for source in range(lax.axis_size(axis))]
    return lax.ppermute(value, axis, pairs)


def prepare_traces(trace, flags):
    values = trace.astype(jnp.float32)
    centred = values - jnp.mean(values, axis=-1, keepdims=True)
    spread = jnp.sqrt(jnp.mean(centred * centred, axis=-1, keepdims=True) + 1e-05)
    return (centred / spread * flags.astype(jnp.float32)[:, None]).astype(jnp.bfloat16)


def make_basis():
    times = jnp.arange(SAMPLES, dtype=jnp.int32)
    bins = FLO + jnp.arange(NFREQ, dtype=jnp.int32)
    phase = bins[:, None] * times[None, :] % SAMPLES
    angle = phase.astype(jnp.float32) * (TWO_PI / SAMPLES)
    table = jnp.stack([jnp.cos(angle), -jnp.sin(angle)], axis=1)
    return table.reshape(2 * NFREQ, SAMPLES).astype(jnp.bfloat16)


def lag_angles(first_bin, count_bins, count_lags):
    lag_ticks = (jnp.arange(count_lags, dtype=jnp.int32) - LAGS // 2) * LAGSTEP
    bins = FLO + first_bin + jnp.arange(count_bins, dtype=jnp.int32)
    phase = bins[None, :] * lag_ticks[:, None] % SAMPLES
    return phase.astype(jnp.float32) * (TWO_PI / SAMPLES)


def rotate_spectra(spectra, angles):
    real_part = spectra[:, :, 0, :].astype(jnp.float32)[None]
    imag_part = spectra[:, :, 1, :].astype(jnp.float32)[None]
    cosine = jnp.cos(angles)[:, None, :, None]
    sine = jnp.sin(angles)[:, None, :, None]
    first = real_part * cosine + imag_part * sine
    second = imag_part * cosine - real_part * sine
    return jnp.stack([first, second], axis=3).astype(jnp.bfloat16)


def keep_value(value):
    return value


def hop_rounds(value, bit):
    return swapped(value, "chan", bit)


def fetch_partners(flat, plan):
    rounds = plan.shape[0]
    depth, width = flat.shape
    bits = lax.axis_size("chan").bit_length() - 1
    partners = jnp.broadcast_to(flat[None], (rounds, depth, width))
    for bit in range(bits):
        needed = jnp.right_shift(plan, bit) & 1 == 1
        moved = lax.cond(jnp.any(needed), partial(hop_rounds, bit=bit), keep_value, partners)
        partners = jnp.where(needed[:, None, None], moved, partners)
    return partners


def on_device_hops(record, flags, plan):
    local_windows, width, samples = record.shape
    scaled = prepare_traces(record, flags)
    basis = make_basis()
    spectra = jnp.einsum("kt,wct->wkc", basis, scaled, preferred_element_type=jnp.float32) * (
        1.0 / math.sqrt(samples)
    )
    spectra = spectra.astype(jnp.bfloat16).reshape(local_windows, NFREQ, 2, width)
    lag_rows = LAGS // lax.axis_size("tm")
    spread = lax.all_to_all(spectra, "tm", split_axis=1, concat_axis=0, tiled=True)
    windows, band_bins = (spread.shape[0], spread.shape[1])
    depth = windows * band_bins * 2
    first_bin = lax.axis_index("tm") * band_bins
    partners = fetch_partners(spread.reshape(depth, width), plan)
    scale_out = 1.0 / math.sqrt(windows * NFREQ)
    angles = lag_angles(first_bin, band_bins, lag_rows * lax.axis_size("tm"))
    turned = rotate_spectra(spread, angles).reshape(lag_rows * lax.axis_size("tm"), depth, width)
    total = lax.psum_scatter(
        jnp.einsum("lka,rkb->lrab", turned, partners, preferred_element_type=jnp.float32)
        * scale_out,
        "tm",
        scatter_dimension=0,
        tiled=True,
    )
    return total.astype(jnp.bfloat16)


MESH = pl.DeviceIdType.MESH
SPLIT = 2


def basis_table():
    times = np.arange(SAMPLES, dtype=np.int64)
    bins = FLO + np.arange(NFREQ, dtype=np.int64)
    angle = (bins[:, None] * times[None, :] % SAMPLES).astype(np.float32) * np.float32(TWO_PI / SAMPLES)
    return np.concatenate([np.cos(angle), -np.sin(angle)], axis=0).astype(jnp.bfloat16)


def angle_table():
    ticks = (np.arange(LAGS, dtype=np.int64) - LAGS // 2) * LAGSTEP
    bins = FLO + np.arange(NFREQ, dtype=np.int64)
    angle = (bins[None, :] * ticks[:, None] % SAMPLES).astype(np.float32) * np.float32(TWO_PI / SAMPLES)
    return np.stack([np.cos(angle), np.sin(angle)], axis=1).astype(np.float32)[..., None]


def kernel(
    lines, plan_ref, flags_ref, trig_ref, basis_hbm, record_hbm, out_ref,
    basis_ref, rec_ref, blocks, turned,
    in_sem, up_sem, down_sem, side_sem, core_sem, recv_sem, core_recv,
):
    group, block, core = lax.axis_index("groups"), lax.axis_index("chan"), lax.axis_index("tm")
    line, side = block // SPLIT, block % SPLIT
    windows, samples, width = rec_ref.shape
    rounds, lag_rows = out_ref.shape[1], out_ref.shape[0]
    rows = 2 * NFREQ
    other = 1 - core

    loads = [pltpu.make_async_copy(basis_hbm, basis_ref, in_sem.at[windows])]
    loads += [pltpu.make_async_copy(record_hbm.at[w], rec_ref.at[w], in_sem.at[w]) for w in range(windows)]
    for load in loads:
        load.start()

    up_id = (group, block + SPLIT, core)
    down_id = (group, block - SPLIT, core)
    side_id = (group, line * SPLIT + (1 - side), core)
    core_id = (group, block, other)
    has_up, has_down = line < lines - 1, line > 0

    barrier = pltpu.get_barrier_semaphore()

    @pl.when(has_up)
    def _():
        pl.semaphore_signal(barrier, inc=1, device_id=up_id, device_id_type=MESH)

    @pl.when(has_down)
    def _():
        pl.semaphore_signal(barrier, inc=1, device_id=down_id, device_id_type=MESH)

    pl.semaphore_signal(barrier, inc=1, device_id=side_id, device_id_type=MESH)
    pl.semaphore_signal(barrier, inc=1, device_id=core_id, device_id_type=MESH)

    def send(slot, w, target, send_sem, arrive):
        piece = blocks.at[slot, core, w]
        return pltpu.make_async_remote_copy(
            src_ref=piece, dst_ref=piece, send_sem=send_sem.at[slot, w], recv_sem=arrive.at[slot, w],
            device_id=target, device_id_type=MESH,
        )

    def up(slot, w):
        return send(slot, w, up_id, up_sem, recv_sem)

    def down(slot, w):
        return send(slot, w, down_id, down_sem, recv_sem)

    def across(slot, w):
        return send(slot, w, side_id, side_sem, recv_sem)

    def share(slot, w):
        return send(slot, w, core_id, core_sem, core_recv)

    def arrived(slot, w):
        across(slot, w).wait_recv()

    tile = 80
    whole = samples // tile * tile
    flag_row = flags_ref[...].astype(jnp.float32) * (1.0 / math.sqrt(samples))
    loads[0].wait()
    row_sums = jnp.sum(basis_ref[...].astype(jnp.float32), axis=-1, keepdims=True)

    def fold(values):
        return jnp.sum(values.reshape(-1, 8, width), axis=0)

    for w in range(windows):
        loads[1 + w].wait()
        spectrum = jnp.dot(basis_ref[...], rec_ref[w], preferred_element_type=jnp.float32)

        def sum_tile(i, carry, w=w):
            at = pl.ds(pl.multiple_of(i * tile, 16), tile)
            return carry + fold(rec_ref[w, at, :].astype(jnp.float32))

        zero = jnp.zeros((8, width), jnp.float32)
        total = lax.fori_loop(0, whole // tile, sum_tile, zero, unroll=4)
        total += fold(rec_ref[w, whole:, :].astype(jnp.float32))
        mean = jnp.sum(total, axis=0, keepdims=True) * (1.0 / samples)

        def power_tile(i, carry, w=w, mean=mean):
            at = pl.ds(pl.multiple_of(i * tile, 16), tile)
            centred = rec_ref[w, at, :].astype(jnp.float32) - mean
            return carry + fold(centred * centred)

        power = lax.fori_loop(0, whole // tile, power_tile, zero, unroll=4)
        centred = rec_ref[w, whole:, :].astype(jnp.float32) - mean
        power += fold(centred * centred)
        power = jnp.sum(power, axis=0, keepdims=True) * (1.0 / samples)
        gain = flag_row * lax.rsqrt(power + 1e-05)
        blocks[block, core, w] = ((spectrum - row_sums * mean) * gain).astype(jnp.bfloat16)
        if w == 0:
            pl.semaphore_wait(barrier, 2 + has_up.astype(jnp.int32) + has_down.astype(jnp.int32))

        @pl.when(has_up)
        def _(w=w):
            up(block, w).start()

        @pl.when(has_down)
        def _(w=w):
            down(block, w).start()

        across(block, w).start()
        share(block, w).start()

    def rotate(half):
        for pair in range(0, windows, 2):
            for lag in range(lag_rows):
                at = core * lag_rows + lag
                cosine, sine = trig_ref[at, 0], trig_ref[at, 1]
                parts = []
                for w in (pair, pair + 1):
                    both = blocks[block, half, w].astype(jnp.float32)
                    real, imag = both[:NFREQ], both[NFREQ:]
                    parts += [real * cosine + imag * sine, imag * cosine - real * sine]
                flipped = jnp.concatenate(parts, axis=0).T
                for h in range(2):
                    @pl.when(half == h)
                    def _():
                        first = h * windows * rows + pair * rows
                        turned[lag * width:(lag + 1) * width, first:first + 2 * rows] = flipped.astype(jnp.bfloat16)

    def take_side(source, ok):
        slot = source * SPLIT + (1 - side)

        @pl.when(ok)
        def _():
            def step(w, _):
                arrived(slot, w)
                share(slot, w).start()
                return 0

            lax.fori_loop(0, windows, step, 0)

    rotate(core)
    for s in range(1, lines):
        from_below, from_above = line >= s, line + s < lines

        def step(w, _, s=s, from_below=from_below, from_above=from_above):
            @pl.when(from_below)
            def _():
                slot = block - s * SPLIT
                arrived(slot, w)

                @pl.when(has_up)
                def _():
                    up(slot, w).start()

                across(slot, w).start()
                share(slot, w).start()

            @pl.when(from_above)
            def _():
                slot = block + s * SPLIT
                arrived(slot, w)

                @pl.when(has_down)
                def _():
                    down(slot, w).start()

                across(slot, w).start()
                share(slot, w).start()

            return 0

        lax.fori_loop(0, windows, step, 0)
        if s == 1:
            take_side(line, line >= 0)
            for w in range(windows):
                share(block, w).wait_recv()
            rotate(other)
        else:
            take_side(line - (s - 1), line >= s - 1)
            take_side(line + (s - 1), line + s - 1 < lines)
    take_side(line - (lines - 1), line >= lines - 1)
    take_side(line + (lines - 1), line < 1)

    def finish(slot, _):
        source, column = slot // SPLIT, slot % SPLIT
        mine = column == side

        def step(w, _):
            share(slot, w).wait_send()

            @pl.when(mine)
            def _():
                across(slot, w).wait_send()

            @pl.when(jnp.logical_and(mine, jnp.logical_and(has_up, source <= line)))
            def _():
                up(slot, w).wait_send()

            @pl.when(jnp.logical_and(mine, jnp.logical_and(has_down, source >= line)))
            def _():
                down(slot, w).wait_send()

            @pl.when(slot != block)
            def _():
                share(slot, w).wait_recv()

            return 0

        lax.fori_loop(0, windows, step, 0)
        return 0

    lax.fori_loop(0, lines * SPLIT, finish, 0)

    scale_out = 1.0 / math.sqrt(2 * windows * NFREQ)
    depth = 2 * windows * rows
    for r in range(rounds):
        partner = blocks[jnp.bitwise_xor(block, plan_ref[r])].reshape(depth, width)
        total = jnp.dot(turned[...], partner, preferred_element_type=jnp.float32) * scale_out
        out_ref[:, r] = total.reshape(lag_rows, width, width).astype(jnp.bfloat16)


def on_device_kernel(record, flags, plan):
    windows, width, samples = record.shape
    blocks = lax.axis_size("chan")
    lines = blocks // SPLIT
    cores = lax.axis_size("tm")
    rows = 2 * NFREQ
    lag_rows = LAGS // cores
    depth = cores * windows * rows
    per_piece = pltpu.SemaphoreType.DMA((blocks, windows))
    return pl.pallas_call(
        partial(kernel, lines),
        out_shape=jax.ShapeDtypeStruct((lag_rows, plan.shape[0], width, width), jnp.bfloat16),
        in_specs=[
            pl.BlockSpec(memory_space=pltpu.SMEM),
            pl.BlockSpec(memory_space=pltpu.VMEM),
            pl.BlockSpec(memory_space=pltpu.VMEM),
            pl.BlockSpec(memory_space=pl.ANY),
            pl.BlockSpec(memory_space=pl.ANY),
        ],
        out_specs=pl.BlockSpec(memory_space=pltpu.VMEM),
        scratch_shapes=[
            pltpu.VMEM((rows, samples), jnp.bfloat16),
            pltpu.VMEM((windows, samples, width), jnp.bfloat16),
            pltpu.VMEM((blocks, cores, windows, rows, width), jnp.bfloat16),
            pltpu.VMEM((lag_rows * width, depth), jnp.bfloat16),
            pltpu.SemaphoreType.DMA((windows + 1,)),
            per_piece, per_piece, per_piece, per_piece, per_piece, per_piece,
        ],
        compiler_params=pltpu.CompilerParams(
            collective_id=0, has_side_effects=True, vmem_limit_bytes=56 * 1024 * 1024
        ),
    )(plan, flags.reshape(1, width), jnp.asarray(angle_table()), jnp.asarray(basis_table()), jnp.swapaxes(record, 1, 2))


def solution(mesh):
    blocks, cores = mesh.shape["chan"], mesh.shape["tm"]
    small = cores == 2 and blocks % SPLIT == 0 and blocks <= 8
    return jax.shard_map(
        on_device_kernel if small else on_device_hops,
        mesh=mesh,
        in_specs=(P("tm", ("groups", "chan"), None), P(("groups", "chan")), P()),
        out_specs=P("tm", None, ("groups", "chan"), None),
        check_vma=False,
    )
```

```python
from functools import partial
import math

import jax
import jax.numpy as jnp
from jax import lax
from jax.experimental import pallas as pl
from jax.experimental.pallas import tpu as pltpu
from jax.sharding import PartitionSpec as P

SAMPLES = 1000
NFREQ = 32
FLO = 5
LAGS = 4
LAGSTEP = 3


TWO_PI = 2.0 * math.pi


def swapped(value, axis, apart):
    mask = 2**apart
    pairs = [(source, source ^ mask) for source in range(lax.axis_size(axis))]
    return lax.ppermute(value, axis, pairs)


def prepare_traces(trace, flags):
    values = trace.astype(jnp.float32)
    centred = values - jnp.mean(values, axis=-1, keepdims=True)
    spread = jnp.sqrt(jnp.mean(centred * centred, axis=-1, keepdims=True) + 1e-05)
    return (centred / spread * flags.astype(jnp.float32)[:, None]).astype(jnp.bfloat16)


def make_basis():
    times = jnp.arange(SAMPLES, dtype=jnp.int32)
    bins = FLO + jnp.arange(NFREQ, dtype=jnp.int32)
    phase = bins[:, None] * times[None, :] % SAMPLES
    angle = phase.astype(jnp.float32) * (TWO_PI / SAMPLES)
    table = jnp.stack([jnp.cos(angle), -jnp.sin(angle)], axis=1)
    return table.reshape(2 * NFREQ, SAMPLES).astype(jnp.bfloat16)


def lag_angles(first_bin, count_bins, count_lags):
    lag_ticks = (jnp.arange(count_lags, dtype=jnp.int32) - LAGS // 2) * LAGSTEP
    bins = FLO + first_bin + jnp.arange(count_bins, dtype=jnp.int32)
    phase = bins[None, :] * lag_ticks[:, None] % SAMPLES
    return phase.astype(jnp.float32) * (TWO_PI / SAMPLES)


def rotate_spectra(spectra, angles):
    real_part = spectra[:, :, 0, :].astype(jnp.float32)[None]
    imag_part = spectra[:, :, 1, :].astype(jnp.float32)[None]
    cosine = jnp.cos(angles)[:, None, :, None]
    sine = jnp.sin(angles)[:, None, :, None]
    first = real_part * cosine + imag_part * sine
    second = imag_part * cosine - real_part * sine
    return jnp.stack([first, second], axis=3).astype(jnp.bfloat16)


def keep_value(value):
    return value


def hop_rounds(value, bit):
    return swapped(value, "chan", bit)


def fetch_partners(flat, plan):
    rounds = plan.shape[0]
    depth, width = flat.shape
    bits = lax.axis_size("chan").bit_length() - 1
    partners = jnp.broadcast_to(flat[None], (rounds, depth, width))
    for bit in range(bits):
        needed = jnp.right_shift(plan, bit) & 1 == 1
        moved = lax.cond(jnp.any(needed), partial(hop_rounds, bit=bit), keep_value, partners)
        partners = jnp.where(needed[:, None, None], moved, partners)
    return partners


def on_device_hops(record, flags, plan):
    local_windows, width, samples = record.shape
    scaled = prepare_traces(record, flags)
    basis = make_basis()
    spectra = jnp.einsum("kt,wct->wkc", basis, scaled, preferred_element_type=jnp.float32) * (
        1.0 / math.sqrt(samples)
    )
    spectra = spectra.astype(jnp.bfloat16).reshape(local_windows, NFREQ, 2, width)
    lag_rows = LAGS // lax.axis_size("tm")
    spread = lax.all_to_all(spectra, "tm", split_axis=1, concat_axis=0, tiled=True)
    windows, band_bins = (spread.shape[0], spread.shape[1])
    depth = windows * band_bins * 2
    first_bin = lax.axis_index("tm") * band_bins
    partners = fetch_partners(spread.reshape(depth, width), plan)
    scale_out = 1.0 / math.sqrt(windows * NFREQ)
    angles = lag_angles(first_bin, band_bins, lag_rows * lax.axis_size("tm"))
    turned = rotate_spectra(spread, angles).reshape(lag_rows * lax.axis_size("tm"), depth, width)
    total = lax.psum_scatter(
        jnp.einsum("lka,rkb->lrab", turned, partners, preferred_element_type=jnp.float32)
        * scale_out,
        "tm",
        scatter_dimension=0,
        tiled=True,
    )
    return total.astype(jnp.bfloat16)


MESH = pl.DeviceIdType.MESH
SPLIT = 2


def cos_sin(ticks):
    near = ticks - SAMPLES * jnp.floor(ticks * (1.0 / SAMPLES) + 0.5)
    angle = near * (TWO_PI / SAMPLES / 4)
    square = angle * angle
    sine = angle * (1 + square * (-1 / 6 + square * (1 / 120 + square * (-1 / 5040 + square * (1 / 362880)))))
    half_sine = 1 - 2 * sine * sine
    cosine = 1 + square * (-1 / 2 + square * (1 / 24 + square * (-1 / 720 + square * (1 / 40320))))
    cosine, sine = half_sine, 2 * sine * cosine
    return 1 - 2 * sine * sine, 2 * sine * cosine


def kernel(
    lines, plan_ref, flags_ref, record_hbm, out_ref,
    basis_ref, rec_ref, blocks, turned,
    in_sem, up_sem, down_sem, side_sem, core_sem, recv_sem, core_recv,
):
    group, block, core = lax.axis_index("groups"), lax.axis_index("chan"), lax.axis_index("tm")
    line, side = block // SPLIT, block % SPLIT
    windows, samples, width = rec_ref.shape
    rounds, lag_rows = out_ref.shape[1], out_ref.shape[0]
    rows = 2 * NFREQ
    other = 1 - core

    loads = [pltpu.make_async_copy(record_hbm.at[w], rec_ref.at[w], in_sem.at[w]) for w in range(windows)]
    for load in loads:
        load.start()

    up_id = (group, block + SPLIT, core)
    down_id = (group, block - SPLIT, core)
    side_id = (group, line * SPLIT + (1 - side), core)
    core_id = (group, block, other)
    has_up, has_down = line < lines - 1, line > 0

    barrier = pltpu.get_barrier_semaphore()

    @pl.when(has_up)
    def _():
        pl.semaphore_signal(barrier, inc=1, device_id=up_id, device_id_type=MESH)

    @pl.when(has_down)
    def _():
        pl.semaphore_signal(barrier, inc=1, device_id=down_id, device_id_type=MESH)

    pl.semaphore_signal(barrier, inc=1, device_id=side_id, device_id_type=MESH)
    pl.semaphore_signal(barrier, inc=1, device_id=core_id, device_id_type=MESH)

    def send(slot, w, target, send_sem, arrive):
        piece = blocks.at[slot, core, w]
        return pltpu.make_async_remote_copy(
            src_ref=piece, dst_ref=piece, send_sem=send_sem.at[slot, w], recv_sem=arrive.at[slot, w],
            device_id=target, device_id_type=MESH,
        )

    def up(slot, w):
        return send(slot, w, up_id, up_sem, recv_sem)

    def down(slot, w):
        return send(slot, w, down_id, down_sem, recv_sem)

    def across(slot, w):
        return send(slot, w, side_id, side_sem, recv_sem)

    def share(slot, w):
        return send(slot, w, core_id, core_sem, core_recv)

    def arrived(slot, w):
        across(slot, w).wait_recv()

    tile = 80
    whole = samples // tile * tile
    flag_row = flags_ref[...].astype(jnp.float32) * (1.0 / math.sqrt(samples))
    bins = FLO + lax.broadcasted_iota(jnp.int32, (NFREQ, samples), 0).astype(jnp.float32)
    times = lax.broadcasted_iota(jnp.int32, (NFREQ, samples), 1).astype(jnp.float32)
    cosine, sine = cos_sin(bins * times)
    basis_ref[:NFREQ, :] = cosine.astype(jnp.bfloat16)
    basis_ref[NFREQ:, :] = (-sine).astype(jnp.bfloat16)
    row_sums = jnp.sum(basis_ref[...].astype(jnp.float32), axis=-1, keepdims=True)

    def fold(values):
        return jnp.sum(values.reshape(-1, 8, width), axis=0)

    for w in range(windows):
        loads[w].wait()
        spectrum = jnp.dot(basis_ref[...], rec_ref[w], preferred_element_type=jnp.float32)

        def sum_tile(i, carry, w=w):
            at = pl.ds(pl.multiple_of(i * tile, 16), tile)
            return carry + fold(rec_ref[w, at, :].astype(jnp.float32))

        zero = jnp.zeros((8, width), jnp.float32)
        total = lax.fori_loop(0, whole // tile, sum_tile, zero, unroll=4)
        total += fold(rec_ref[w, whole:, :].astype(jnp.float32))
        mean = jnp.sum(total, axis=0, keepdims=True) * (1.0 / samples)

        def power_tile(i, carry, w=w, mean=mean):
            at = pl.ds(pl.multiple_of(i * tile, 16), tile)
            centred = rec_ref[w, at, :].astype(jnp.float32) - mean
            return carry + fold(centred * centred)

        power = lax.fori_loop(0, whole // tile, power_tile, zero, unroll=4)
        centred = rec_ref[w, whole:, :].astype(jnp.float32) - mean
        power += fold(centred * centred)
        power = jnp.sum(power, axis=0, keepdims=True) * (1.0 / samples)
        gain = flag_row * lax.rsqrt(power + 1e-05)
        blocks[block, core, w] = ((spectrum - row_sums * mean) * gain).astype(jnp.bfloat16)
        if w == 0:
            pl.semaphore_wait(barrier, 2 + has_up.astype(jnp.int32) + has_down.astype(jnp.int32))

        @pl.when(has_up)
        def _(w=w):
            up(block, w).start()

        @pl.when(has_down)
        def _(w=w):
            down(block, w).start()

        across(block, w).start()
        share(block, w).start()

    def rotate(half):
        for pair in range(0, windows, 2):
            for lag in range(lag_rows):
                tick = ((core * lag_rows + lag - LAGS // 2) * LAGSTEP).astype(jnp.float32)
                bins = FLO + lax.broadcasted_iota(jnp.int32, (NFREQ, width), 0).astype(jnp.float32)
                cosine, sine = cos_sin(bins * tick)
                parts = []
                for w in (pair, pair + 1):
                    both = blocks[block, half, w].astype(jnp.float32)
                    real, imag = both[:NFREQ], both[NFREQ:]
                    parts += [real * cosine + imag * sine, imag * cosine - real * sine]
                flipped = jnp.concatenate(parts, axis=0).T
                for h in range(2):
                    @pl.when(half == h)
                    def _():
                        first = h * windows * rows + pair * rows
                        turned[lag * width:(lag + 1) * width, first:first + 2 * rows] = flipped.astype(jnp.bfloat16)

    def take_side(source, ok):
        slot = source * SPLIT + (1 - side)

        @pl.when(ok)
        def _():
            def step(w, _):
                arrived(slot, w)
                share(slot, w).start()
                return 0

            lax.fori_loop(0, windows, step, 0)

    rotate(core)
    for s in range(1, lines):
        from_below, from_above = line >= s, line + s < lines

        def step(w, _, s=s, from_below=from_below, from_above=from_above):
            @pl.when(from_below)
            def _():
                slot = block - s * SPLIT
                arrived(slot, w)

                @pl.when(has_up)
                def _():
                    up(slot, w).start()

                across(slot, w).start()
                share(slot, w).start()

            @pl.when(from_above)
            def _():
                slot = block + s * SPLIT
                arrived(slot, w)

                @pl.when(has_down)
                def _():
                    down(slot, w).start()

                across(slot, w).start()
                share(slot, w).start()

            return 0

        lax.fori_loop(0, windows, step, 0)
        if s == 1:
            take_side(line, line >= 0)
        else:
            take_side(line - (s - 1), line >= s - 1)
            take_side(line + (s - 1), line + s - 1 < lines)
    for w in range(windows):
        share(block, w).wait_recv()
    rotate(other)
    take_side(line - (lines - 1), line >= lines - 1)
    take_side(line + (lines - 1), line < 1)

    def finish(slot, _):
        source, column = slot // SPLIT, slot % SPLIT
        mine = column == side

        def step(w, _):
            share(slot, w).wait_send()

            @pl.when(mine)
            def _():
                across(slot, w).wait_send()

            @pl.when(jnp.logical_and(mine, jnp.logical_and(has_up, source <= line)))
            def _():
                up(slot, w).wait_send()

            @pl.when(jnp.logical_and(mine, jnp.logical_and(has_down, source >= line)))
            def _():
                down(slot, w).wait_send()

            @pl.when(slot != block)
            def _():
                share(slot, w).wait_recv()

            return 0

        lax.fori_loop(0, windows, step, 0)
        return 0

    lax.fori_loop(0, lines * SPLIT, finish, 0)

    scale_out = 1.0 / math.sqrt(2 * windows * NFREQ)
    depth = 2 * windows * rows
    for r in range(rounds):
        partner = blocks[jnp.bitwise_xor(block, plan_ref[r])].reshape(depth, width)
        total = jnp.dot(turned[...], partner, preferred_element_type=jnp.float32) * scale_out
        out_ref[:, r] = total.reshape(lag_rows, width, width).astype(jnp.bfloat16)


def on_device_kernel(record, flags, plan):
    windows, width, samples = record.shape
    blocks = lax.axis_size("chan")
    lines = blocks // SPLIT
    cores = lax.axis_size("tm")
    rows = 2 * NFREQ
    lag_rows = LAGS // cores
    depth = cores * windows * rows
    per_piece = pltpu.SemaphoreType.DMA((blocks, windows))
    return pl.pallas_call(
        partial(kernel, lines),
        out_shape=jax.ShapeDtypeStruct((lag_rows, plan.shape[0], width, width), jnp.bfloat16),
        in_specs=[
            pl.BlockSpec(memory_space=pltpu.SMEM),
            pl.BlockSpec(memory_space=pltpu.VMEM),
            pl.BlockSpec(memory_space=pl.ANY),
        ],
        out_specs=pl.BlockSpec(memory_space=pltpu.VMEM),
        scratch_shapes=[
            pltpu.VMEM((rows, samples), jnp.bfloat16),
            pltpu.VMEM((windows, samples, width), jnp.bfloat16),
            pltpu.VMEM((blocks, cores, windows, rows, width), jnp.bfloat16),
            pltpu.VMEM((lag_rows * width, depth), jnp.bfloat16),
            pltpu.SemaphoreType.DMA((windows,)),
            per_piece, per_piece, per_piece, per_piece, per_piece, per_piece,
        ],
        compiler_params=pltpu.CompilerParams(
            collective_id=0, has_side_effects=True, vmem_limit_bytes=52 * 1024 * 1024
        ),
    )(plan, flags.reshape(1, width), jnp.swapaxes(record, 1, 2))


def solution(mesh):
    blocks, cores = mesh.shape["chan"], mesh.shape["tm"]
    small = cores == 2 and blocks % SPLIT == 0 and blocks <= 8
    return jax.shard_map(
        on_device_kernel if small else on_device_hops,
        mesh=mesh,
        in_specs=(P("tm", ("groups", "chan"), None), P(("groups", "chan")), P()),
        out_specs=P("tm", None, ("groups", "chan"), None),
        check_vma=False,
    )
```

```python
from functools import partial
import math

import jax
import jax.numpy as jnp
import numpy as np
from jax import lax
from jax.experimental import pallas as pl
from jax.experimental.pallas import tpu as pltpu
from jax.sharding import PartitionSpec as P

SAMPLES = 1000
NFREQ = 32
FLO = 5
LAGS = 4
LAGSTEP = 3


TWO_PI = 2.0 * math.pi


def swapped(value, axis, apart):
    mask = 2**apart
    pairs = [(source, source ^ mask) for source in range(lax.axis_size(axis))]
    return lax.ppermute(value, axis, pairs)


def prepare_traces(trace, flags):
    values = trace.astype(jnp.float32)
    centred = values - jnp.mean(values, axis=-1, keepdims=True)
    spread = jnp.sqrt(jnp.mean(centred * centred, axis=-1, keepdims=True) + 1e-05)
    return (centred / spread * flags.astype(jnp.float32)[:, None]).astype(jnp.bfloat16)


def make_basis():
    times = jnp.arange(SAMPLES, dtype=jnp.int32)
    bins = FLO + jnp.arange(NFREQ, dtype=jnp.int32)
    phase = bins[:, None] * times[None, :] % SAMPLES
    angle = phase.astype(jnp.float32) * (TWO_PI / SAMPLES)
    table = jnp.stack([jnp.cos(angle), -jnp.sin(angle)], axis=1)
    return table.reshape(2 * NFREQ, SAMPLES).astype(jnp.bfloat16)


def lag_angles(first_bin, count_bins, count_lags):
    lag_ticks = (jnp.arange(count_lags, dtype=jnp.int32) - LAGS // 2) * LAGSTEP
    bins = FLO + first_bin + jnp.arange(count_bins, dtype=jnp.int32)
    phase = bins[None, :] * lag_ticks[:, None] % SAMPLES
    return phase.astype(jnp.float32) * (TWO_PI / SAMPLES)


def rotate_spectra(spectra, angles):
    real_part = spectra[:, :, 0, :].astype(jnp.float32)[None]
    imag_part = spectra[:, :, 1, :].astype(jnp.float32)[None]
    cosine = jnp.cos(angles)[:, None, :, None]
    sine = jnp.sin(angles)[:, None, :, None]
    first = real_part * cosine + imag_part * sine
    second = imag_part * cosine - real_part * sine
    return jnp.stack([first, second], axis=3).astype(jnp.bfloat16)


def keep_value(value):
    return value


def hop_rounds(value, bit):
    return swapped(value, "chan", bit)


def fetch_partners(flat, plan):
    rounds = plan.shape[0]
    depth, width = flat.shape
    bits = lax.axis_size("chan").bit_length() - 1
    partners = jnp.broadcast_to(flat[None], (rounds, depth, width))
    for bit in range(bits):
        needed = jnp.right_shift(plan, bit) & 1 == 1
        moved = lax.cond(jnp.any(needed), partial(hop_rounds, bit=bit), keep_value, partners)
        partners = jnp.where(needed[:, None, None], moved, partners)
    return partners


def on_device_hops(record, flags, plan):
    local_windows, width, samples = record.shape
    scaled = prepare_traces(record, flags)
    basis = make_basis()
    spectra = jnp.einsum("kt,wct->wkc", basis, scaled, preferred_element_type=jnp.float32) * (
        1.0 / math.sqrt(samples)
    )
    spectra = spectra.astype(jnp.bfloat16).reshape(local_windows, NFREQ, 2, width)
    lag_rows = LAGS // lax.axis_size("tm")
    spread = lax.all_to_all(spectra, "tm", split_axis=1, concat_axis=0, tiled=True)
    windows, band_bins = (spread.shape[0], spread.shape[1])
    depth = windows * band_bins * 2
    first_bin = lax.axis_index("tm") * band_bins
    partners = fetch_partners(spread.reshape(depth, width), plan)
    scale_out = 1.0 / math.sqrt(windows * NFREQ)
    angles = lag_angles(first_bin, band_bins, lag_rows * lax.axis_size("tm"))
    turned = rotate_spectra(spread, angles).reshape(lag_rows * lax.axis_size("tm"), depth, width)
    total = lax.psum_scatter(
        jnp.einsum("lka,rkb->lrab", turned, partners, preferred_element_type=jnp.float32)
        * scale_out,
        "tm",
        scatter_dimension=0,
        tiled=True,
    )
    return total.astype(jnp.bfloat16)


MESH = pl.DeviceIdType.MESH
SPLIT = 2


def cos_sin(ticks):
    near = ticks - SAMPLES * jnp.floor(ticks * (1.0 / SAMPLES) + 0.5)
    angle = near * (TWO_PI / SAMPLES / 4)
    square = angle * angle
    sine = angle * (1 + square * (-1 / 6 + square * (1 / 120 + square * (-1 / 5040 + square * (1 / 362880)))))
    half_sine = 1 - 2 * sine * sine
    cosine = 1 + square * (-1 / 2 + square * (1 / 24 + square * (-1 / 720 + square * (1 / 40320))))
    cosine, sine = half_sine, 2 * sine * cosine
    return 1 - 2 * sine * sine, 2 * sine * cosine


def kernel(
    lines, plan_ref, flags_ref, record_hbm, out_ref,
    basis_ref, rec_ref, blocks, turned,
    in_sem, up_sem, down_sem, side_sem, core_sem, recv_sem, core_recv, own_recv,
):
    group, block, core = lax.axis_index("groups"), lax.axis_index("chan"), lax.axis_index("tm")
    line, side = block // SPLIT, block % SPLIT
    windows, samples, width = rec_ref.shape
    rounds, lag_rows = out_ref.shape[1], out_ref.shape[0]
    rows = 2 * NFREQ
    other = 1 - core

    loads = [pltpu.make_async_copy(record_hbm.at[w], rec_ref.at[w], in_sem.at[w]) for w in range(windows)]
    for load in loads:
        load.start()

    up_id = (group, block + SPLIT, core)
    down_id = (group, block - SPLIT, core)
    side_id = (group, line * SPLIT + (1 - side), core)
    core_id = (group, block, other)
    has_up, has_down = line < lines - 1, line > 0

    barrier = pltpu.get_barrier_semaphore()

    @pl.when(has_up)
    def _():
        pl.semaphore_signal(barrier, inc=1, device_id=up_id, device_id_type=MESH)

    @pl.when(has_down)
    def _():
        pl.semaphore_signal(barrier, inc=1, device_id=down_id, device_id_type=MESH)

    pl.semaphore_signal(barrier, inc=1, device_id=side_id, device_id_type=MESH)
    pl.semaphore_signal(barrier, inc=1, device_id=core_id, device_id_type=MESH)

    def send(slot, w, target, send_sem, arrive):
        piece = blocks.at[slot, core, w]
        return pltpu.make_async_remote_copy(
            src_ref=piece, dst_ref=piece, send_sem=send_sem, recv_sem=arrive,
            device_id=target, device_id_type=MESH,
        )

    def up(slot, w):
        return send(slot, w, up_id, up_sem, recv_sem.at[slot, w])

    def down(slot, w):
        return send(slot, w, down_id, down_sem, recv_sem.at[slot, w])

    def across(slot, w):
        return send(slot, w, side_id, side_sem, recv_sem.at[slot, w])

    def share(slot, w):
        return send(slot, w, core_id, core_sem, core_recv)

    def share_own(slot, w):
        return send(slot, w, core_id, core_sem, own_recv)

    def arrived(slot, w):
        across(slot, w).wait_recv()

    tile = 80
    whole = samples // tile * tile
    flag_row = flags_ref[...].astype(jnp.float32) * (1.0 / math.sqrt(samples))
    bins = FLO + lax.broadcasted_iota(jnp.int32, (NFREQ, samples), 0).astype(jnp.float32)
    times = lax.broadcasted_iota(jnp.int32, (NFREQ, samples), 1).astype(jnp.float32)
    cosine, sine = cos_sin(bins * times)
    basis_ref[:NFREQ, :] = cosine.astype(jnp.bfloat16)
    basis_ref[NFREQ:, :] = (-sine).astype(jnp.bfloat16)
    row_sums = jnp.sum(basis_ref[...].astype(jnp.float32), axis=-1, keepdims=True)

    def fold(values):
        return jnp.sum(values.reshape(-1, 8, width), axis=0)

    for w in range(windows):
        loads[w].wait()
        spectrum = jnp.dot(basis_ref[...], rec_ref[w], preferred_element_type=jnp.float32)

        def sum_tile(i, carry, w=w):
            at = pl.ds(pl.multiple_of(i * tile, 16), tile)
            return carry + fold(rec_ref[w, at, :].astype(jnp.float32))

        zero = jnp.zeros((8, width), jnp.float32)
        total = lax.fori_loop(0, whole // tile, sum_tile, zero, unroll=4)
        total += fold(rec_ref[w, whole:, :].astype(jnp.float32))
        mean = jnp.sum(total, axis=0, keepdims=True) * (1.0 / samples)

        def power_tile(i, carry, w=w, mean=mean):
            at = pl.ds(pl.multiple_of(i * tile, 16), tile)
            centred = rec_ref[w, at, :].astype(jnp.float32) - mean
            return carry + fold(centred * centred)

        power = lax.fori_loop(0, whole // tile, power_tile, zero, unroll=4)
        centred = rec_ref[w, whole:, :].astype(jnp.float32) - mean
        power += fold(centred * centred)
        power = jnp.sum(power, axis=0, keepdims=True) * (1.0 / samples)
        gain = flag_row * lax.rsqrt(power + 1e-05)
        blocks[block, core, w] = ((spectrum - row_sums * mean) * gain).astype(jnp.bfloat16)
        if w == 0:
            pl.semaphore_wait(barrier, 2 + has_up.astype(jnp.int32) + has_down.astype(jnp.int32))

        @pl.when(has_up)
        def _(w=w):
            up(block, w).start()

        @pl.when(has_down)
        def _(w=w):
            down(block, w).start()

        across(block, w).start()
        share_own(block, w).start()

    def rotate(half):
        for pair in range(0, windows, 2):
            for lag in range(lag_rows):
                tick = ((core * lag_rows + lag - LAGS // 2) * LAGSTEP).astype(jnp.float32)
                bins = FLO + lax.broadcasted_iota(jnp.int32, (NFREQ, width), 0).astype(jnp.float32)
                cosine, sine = cos_sin(bins * tick)
                parts = []
                for w in (pair, pair + 1):
                    both = blocks[block, half, w].astype(jnp.float32)
                    real, imag = both[:NFREQ], both[NFREQ:]
                    parts += [real * cosine + imag * sine, imag * cosine - real * sine]
                flipped = jnp.concatenate(parts, axis=0).T
                for h in range(2):
                    @pl.when(half == h)
                    def _():
                        first = h * windows * rows + pair * rows
                        turned[lag * width:(lag + 1) * width, first:first + 2 * rows] = flipped.astype(jnp.bfloat16)

    def take_side(source, ok, w):
        slot = source * SPLIT + (1 - side)

        @pl.when(ok)
        def _():
            arrived(slot, w)
            share(slot, w).start()

    def take_line(source, ok, has_next, onward, w):
        @pl.when(ok)
        def _():
            slot = source * SPLIT + side
            arrived(slot, w)

            @pl.when(has_next)
            def _():
                onward(slot, w).start()

            across(slot, w).start()
            share(slot, w).start()

    rotate(core)
    for s in range(1, lines):
        def step(w, _, s=s):
            take_line(line - s, line >= s, has_up, up, w)
            take_line(line + s, line + s < lines, has_down, down, w)
            if s == 2:
                take_side(line, line >= 0, w)
            if s > 2:
                take_side(line - (s - 2), line >= s - 2, w)
                take_side(line + (s - 2), line + s - 2 < lines, w)
            return 0

        lax.fori_loop(0, windows, step, 0)

    def pieces(first, count, sem):
        some = blocks.at[pl.ds(first, count), core]
        return pltpu.make_async_copy(some, some, sem)

    pieces(0, 1, own_recv).wait()
    rotate(other)
    for s in range(max(lines - 2, 0), lines):
        def last(w, _, s=s):
            take_side(line - s, line >= s, w)
            if s > 0:
                take_side(line + s, line + s < lines, w)
            return 0

        lax.fori_loop(0, windows, last, 0)

    pieces(0, lines, side_sem).wait()
    for s in range(lines):
        @pl.when(jnp.logical_and(has_up, line >= s))
        def _():
            pieces(0, 1, up_sem).wait()

        @pl.when(jnp.logical_and(has_down, line + s < lines))
        def _():
            pieces(0, 1, down_sem).wait()

    pieces(0, lines * SPLIT, core_sem).wait()
    pieces(0, lines * SPLIT - 1, core_recv).wait()

    scale_out = 1.0 / math.sqrt(2 * windows * NFREQ)
    depth = 2 * windows * rows
    for r in range(rounds):
        partner = blocks[jnp.bitwise_xor(block, plan_ref[r])].reshape(depth, width)
        total = jnp.dot(turned[...], partner, preferred_element_type=jnp.float32) * scale_out
        out_ref[:, r] = total.reshape(lag_rows, width, width).astype(jnp.bfloat16)


def on_device_kernel(record, flags, plan):
    windows, width, samples = record.shape
    blocks = lax.axis_size("chan")
    lines = blocks // SPLIT
    cores = lax.axis_size("tm")
    rows = 2 * NFREQ
    lag_rows = LAGS // cores
    depth = cores * windows * rows
    per_piece = pltpu.SemaphoreType.DMA((blocks, windows))
    plain = pltpu.SemaphoreType.DMA
    return pl.pallas_call(
        partial(kernel, lines),
        out_shape=jax.ShapeDtypeStruct((lag_rows, plan.shape[0], width, width), jnp.bfloat16),
        in_specs=[
            pl.BlockSpec(memory_space=pltpu.SMEM),
            pl.BlockSpec(memory_space=pltpu.VMEM),
            pl.BlockSpec(memory_space=pl.ANY),
        ],
        out_specs=pl.BlockSpec(memory_space=pltpu.VMEM),
        scratch_shapes=[
            pltpu.VMEM((rows, samples), jnp.bfloat16),
            pltpu.VMEM((windows, samples, width), jnp.bfloat16),
            pltpu.VMEM((blocks, cores, windows, rows, width), jnp.bfloat16),
            pltpu.VMEM((lag_rows * width, depth), jnp.bfloat16),
            pltpu.SemaphoreType.DMA((windows,)),
            plain, plain, plain, plain, per_piece, plain, plain,
        ],
        compiler_params=pltpu.CompilerParams(
            collective_id=0, has_side_effects=True, vmem_limit_bytes=52 * 1024 * 1024
        ),
    )(plan, flags.reshape(1, width), jnp.swapaxes(record, 1, 2))


def solution(mesh):
    blocks, cores = mesh.shape["chan"], mesh.shape["tm"]
    small = cores == 2 and blocks % SPLIT == 0 and blocks <= 4 * SPLIT
    return jax.shard_map(
        on_device_kernel if small else on_device_hops,
        mesh=mesh,
        in_specs=(P("tm", ("groups", "chan"), None), P(("groups", "chan")), P()),
        out_specs=P("tm", None, ("groups", "chan"), None),
        check_vma=False,
    )
```

```python
from functools import partial
import math

import jax
import jax.numpy as jnp
import numpy as np
from jax import lax
from jax.experimental import pallas as pl
from jax.experimental.pallas import tpu as pltpu
from jax.sharding import PartitionSpec as P

SAMPLES = 1000
NFREQ = 32
FLO = 5
LAGS = 4
LAGSTEP = 3


TWO_PI = 2.0 * math.pi


def swapped(value, axis, apart):
    mask = 2**apart
    pairs = [(source, source ^ mask) for source in range(lax.axis_size(axis))]
    return lax.ppermute(value, axis, pairs)


def prepare_traces(trace, flags):
    values = trace.astype(jnp.float32)
    centred = values - jnp.mean(values, axis=-1, keepdims=True)
    spread = jnp.sqrt(jnp.mean(centred * centred, axis=-1, keepdims=True) + 1e-05)
    return (centred / spread * flags.astype(jnp.float32)[:, None]).astype(jnp.bfloat16)


def make_basis():
    times = jnp.arange(SAMPLES, dtype=jnp.int32)
    bins = FLO + jnp.arange(NFREQ, dtype=jnp.int32)
    phase = bins[:, None] * times[None, :] % SAMPLES
    angle = phase.astype(jnp.float32) * (TWO_PI / SAMPLES)
    table = jnp.stack([jnp.cos(angle), -jnp.sin(angle)], axis=1)
    return table.reshape(2 * NFREQ, SAMPLES).astype(jnp.bfloat16)


def lag_angles(first_bin, count_bins, count_lags):
    lag_ticks = (jnp.arange(count_lags, dtype=jnp.int32) - LAGS // 2) * LAGSTEP
    bins = FLO + first_bin + jnp.arange(count_bins, dtype=jnp.int32)
    phase = bins[None, :] * lag_ticks[:, None] % SAMPLES
    return phase.astype(jnp.float32) * (TWO_PI / SAMPLES)


def rotate_spectra(spectra, angles):
    real_part = spectra[:, :, 0, :].astype(jnp.float32)[None]
    imag_part = spectra[:, :, 1, :].astype(jnp.float32)[None]
    cosine = jnp.cos(angles)[:, None, :, None]
    sine = jnp.sin(angles)[:, None, :, None]
    first = real_part * cosine + imag_part * sine
    second = imag_part * cosine - real_part * sine
    return jnp.stack([first, second], axis=3).astype(jnp.bfloat16)


def keep_value(value):
    return value


def hop_rounds(value, bit):
    return swapped(value, "chan", bit)


def fetch_partners(flat, plan):
    rounds = plan.shape[0]
    depth, width = flat.shape
    bits = lax.axis_size("chan").bit_length() - 1
    partners = jnp.broadcast_to(flat[None], (rounds, depth, width))
    for bit in range(bits):
        needed = jnp.right_shift(plan, bit) & 1 == 1
        moved = lax.cond(jnp.any(needed), partial(hop_rounds, bit=bit), keep_value, partners)
        partners = jnp.where(needed[:, None, None], moved, partners)
    return partners


def on_device_hops(record, flags, plan):
    local_windows, width, samples = record.shape
    scaled = prepare_traces(record, flags)
    basis = make_basis()
    spectra = jnp.einsum("kt,wct->wkc", basis, scaled, preferred_element_type=jnp.float32) * (
        1.0 / math.sqrt(samples)
    )
    spectra = spectra.astype(jnp.bfloat16).reshape(local_windows, NFREQ, 2, width)
    lag_rows = LAGS // lax.axis_size("tm")
    spread = lax.all_to_all(spectra, "tm", split_axis=1, concat_axis=0, tiled=True)
    windows, band_bins = (spread.shape[0], spread.shape[1])
    depth = windows * band_bins * 2
    first_bin = lax.axis_index("tm") * band_bins
    partners = fetch_partners(spread.reshape(depth, width), plan)
    scale_out = 1.0 / math.sqrt(windows * NFREQ)
    angles = lag_angles(first_bin, band_bins, lag_rows * lax.axis_size("tm"))
    turned = rotate_spectra(spread, angles).reshape(lag_rows * lax.axis_size("tm"), depth, width)
    total = lax.psum_scatter(
        jnp.einsum("lka,rkb->lrab", turned, partners, preferred_element_type=jnp.float32)
        * scale_out,
        "tm",
        scatter_dimension=0,
        tiled=True,
    )
    return total.astype(jnp.bfloat16)


MESH = pl.DeviceIdType.MESH
SPLIT = 2


def cos_sin(ticks):
    near = ticks - SAMPLES * jnp.floor(ticks * (1.0 / SAMPLES) + 0.5)
    angle = near * (TWO_PI / SAMPLES / 4)
    square = angle * angle
    sine = angle * (1 + square * (-1 / 6 + square * (1 / 120 + square * (-1 / 5040 + square * (1 / 362880)))))
    half_sine = 1 - 2 * sine * sine
    cosine = 1 + square * (-1 / 2 + square * (1 / 24 + square * (-1 / 720 + square * (1 / 40320))))
    cosine, sine = half_sine, 2 * sine * cosine
    return 1 - 2 * sine * sine, 2 * sine * cosine


def kernel(
    lines, plan_ref, flags_ref, record_hbm, out_ref,
    basis_ref, rec_ref, blocks, turned,
    in_sem, up_sem, down_sem, side_sem, core_sem, recv_sem, core_recv, own_recv,
):
    group, block, core = lax.axis_index("groups"), lax.axis_index("chan"), lax.axis_index("tm")
    line, side = block // SPLIT, block % SPLIT
    windows, samples, width = rec_ref.shape
    rounds, lag_rows = out_ref.shape[1], out_ref.shape[0]
    rows = 2 * NFREQ
    other = 1 - core

    loads = [pltpu.make_async_copy(record_hbm.at[w], rec_ref.at[w], in_sem.at[w]) for w in range(windows)]
    for load in loads:
        load.start()

    up_id = (group, block + SPLIT, core)
    down_id = (group, block - SPLIT, core)
    side_id = (group, line * SPLIT + (1 - side), core)
    core_id = (group, block, other)
    has_up, has_down = line < lines - 1, line > 0

    barrier = pltpu.get_barrier_semaphore()

    @pl.when(has_up)
    def _():
        pl.semaphore_signal(barrier, inc=1, device_id=up_id, device_id_type=MESH)

    @pl.when(has_down)
    def _():
        pl.semaphore_signal(barrier, inc=1, device_id=down_id, device_id_type=MESH)

    pl.semaphore_signal(barrier, inc=1, device_id=side_id, device_id_type=MESH)
    pl.semaphore_signal(barrier, inc=1, device_id=core_id, device_id_type=MESH)

    def send(slot, w, target, send_sem, arrive):
        piece = blocks.at[slot, core, w]
        return pltpu.make_async_remote_copy(
            src_ref=piece, dst_ref=piece, send_sem=send_sem, recv_sem=arrive,
            device_id=target, device_id_type=MESH,
        )

    def up(slot, w):
        return send(slot, w, up_id, up_sem, recv_sem.at[slot, w])

    def down(slot, w):
        return send(slot, w, down_id, down_sem, recv_sem.at[slot, w])

    def across(slot, w):
        return send(slot, w, side_id, side_sem, recv_sem.at[slot, w])

    def share(slot, w):
        return send(slot, w, core_id, core_sem, core_recv)

    def share_own(slot, w):
        return send(slot, w, core_id, core_sem, own_recv)

    def arrived(slot, w):
        across(slot, w).wait_recv()

    tile = 80
    whole = samples // tile * tile
    flag_row = flags_ref[...].astype(jnp.float32) * (1.0 / math.sqrt(samples))
    bins = FLO + lax.broadcasted_iota(jnp.int32, (NFREQ, samples), 0).astype(jnp.float32)
    times = lax.broadcasted_iota(jnp.int32, (NFREQ, samples), 1).astype(jnp.float32)
    cosine, sine = cos_sin(bins * times)
    basis_ref[:NFREQ, :] = cosine.astype(jnp.bfloat16)
    basis_ref[NFREQ:, :] = (-sine).astype(jnp.bfloat16)
    row_sums = jnp.sum(basis_ref[...].astype(jnp.float32), axis=-1, keepdims=True)

    def fold(values):
        return jnp.sum(values.reshape(-1, 8, width), axis=0)

    for w in range(windows):
        loads[w].wait()
        spectrum = jnp.dot(basis_ref[...], rec_ref[w], preferred_element_type=jnp.float32)

        def sum_tile(i, carry, w=w):
            at = pl.ds(pl.multiple_of(i * tile, 16), tile)
            return carry + fold(rec_ref[w, at, :].astype(jnp.float32))

        zero = jnp.zeros((8, width), jnp.float32)
        total = lax.fori_loop(0, whole // tile, sum_tile, zero, unroll=4)
        total += fold(rec_ref[w, whole:, :].astype(jnp.float32))
        mean = jnp.sum(total, axis=0, keepdims=True) * (1.0 / samples)

        def power_tile(i, carry, w=w, mean=mean):
            at = pl.ds(pl.multiple_of(i * tile, 16), tile)
            centred = rec_ref[w, at, :].astype(jnp.float32) - mean
            return carry + fold(centred * centred)

        power = lax.fori_loop(0, whole // tile, power_tile, zero, unroll=4)
        centred = rec_ref[w, whole:, :].astype(jnp.float32) - mean
        power += fold(centred * centred)
        power = jnp.sum(power, axis=0, keepdims=True) * (1.0 / samples)
        gain = flag_row * lax.rsqrt(power + 1e-05)
        spectrum = ((spectrum - row_sums * mean) * gain).astype(jnp.bfloat16)
        blocks[block, core, 2 * w] = spectrum[:NFREQ]
        blocks[block, core, 2 * w + 1] = spectrum[NFREQ:]
        if w == 0:
            pl.semaphore_wait(barrier, 2 + has_up.astype(jnp.int32) + has_down.astype(jnp.int32))

        for part in (2 * w, 2 * w + 1):
            @pl.when(has_up)
            def _():
                up(block, part).start()

            @pl.when(has_down)
            def _():
                down(block, part).start()

            across(block, part).start()
            share_own(block, part).start()

    def rotate(half):
        for pair in range(0, windows, 2):
            for lag in range(lag_rows):
                tick = ((core * lag_rows + lag - LAGS // 2) * LAGSTEP).astype(jnp.float32)
                bins = FLO + lax.broadcasted_iota(jnp.int32, (NFREQ, width), 0).astype(jnp.float32)
                cosine, sine = cos_sin(bins * tick)
                parts = []
                for w in (pair, pair + 1):
                    real = blocks[block, half, 2 * w].astype(jnp.float32)
                    imag = blocks[block, half, 2 * w + 1].astype(jnp.float32)
                    parts += [real * cosine + imag * sine, imag * cosine - real * sine]
                flipped = jnp.concatenate(parts, axis=0).T
                for h in range(2):
                    @pl.when(half == h)
                    def _():
                        first = h * windows * rows + pair * rows
                        turned[lag * width:(lag + 1) * width, first:first + 2 * rows] = flipped.astype(jnp.bfloat16)

    def take_side(source, ok, w):
        slot = source * SPLIT + (1 - side)

        @pl.when(ok)
        def _():
            arrived(slot, w)
            share(slot, w).start()

    def take_line(source, ok, has_next, onward, w):
        @pl.when(ok)
        def _():
            slot = source * SPLIT + side
            arrived(slot, w)

            @pl.when(has_next)
            def _():
                onward(slot, w).start()

            across(slot, w).start()
            share(slot, w).start()

    def pieces(first, count, sem):
        some = blocks.at[pl.ds(first, count), core]
        return pltpu.make_async_copy(some, some, sem)

    rotate(core)
    for s in range(1, lines):
        def step(w, _, s=s):
            take_line(line - s, line >= s, has_up, up, w)
            take_line(line + s, line + s < lines, has_down, down, w)
            if s == 2:
                take_side(line, line >= 0, w)
            if s > 2:
                take_side(line - (s - 2), line >= s - 2, w)
                take_side(line + (s - 2), line + s - 2 < lines, w)
            return 0

        if s == lines - 1:
            pieces(0, 1, own_recv).wait()
            rotate(other)
        lax.fori_loop(0, 2 * windows, step, 0)

    for s in range(max(lines - 2, 0), lines):
        def last(w, _, s=s):
            take_side(line - s, line >= s, w)
            if s > 0:
                take_side(line + s, line + s < lines, w)
            return 0

        lax.fori_loop(0, 2 * windows, last, 0)

    pieces(0, lines, side_sem).wait()
    for s in range(lines):
        @pl.when(jnp.logical_and(has_up, line >= s))
        def _():
            pieces(0, 1, up_sem).wait()

        @pl.when(jnp.logical_and(has_down, line + s < lines))
        def _():
            pieces(0, 1, down_sem).wait()

    pieces(0, lines * SPLIT, core_sem).wait()
    pieces(0, lines * SPLIT - 1, core_recv).wait()

    scale_out = 1.0 / math.sqrt(2 * windows * NFREQ)
    depth = 2 * windows * rows
    for r in range(rounds):
        partner = blocks[jnp.bitwise_xor(block, plan_ref[r])].reshape(depth, width)
        total = jnp.dot(turned[...], partner, preferred_element_type=jnp.float32) * scale_out
        out_ref[:, r] = total.reshape(lag_rows, width, width).astype(jnp.bfloat16)


def on_device_kernel(record, flags, plan):
    windows, width, samples = record.shape
    blocks = lax.axis_size("chan")
    lines = blocks // SPLIT
    cores = lax.axis_size("tm")
    rows = 2 * NFREQ
    lag_rows = LAGS // cores
    depth = cores * windows * rows
    per_piece = pltpu.SemaphoreType.DMA((blocks, 2 * windows))
    plain = pltpu.SemaphoreType.DMA
    return pl.pallas_call(
        partial(kernel, lines),
        out_shape=jax.ShapeDtypeStruct((lag_rows, plan.shape[0], width, width), jnp.bfloat16),
        in_specs=[
            pl.BlockSpec(memory_space=pltpu.SMEM),
            pl.BlockSpec(memory_space=pltpu.VMEM),
            pl.BlockSpec(memory_space=pl.ANY),
        ],
        out_specs=pl.BlockSpec(memory_space=pltpu.VMEM),
        scratch_shapes=[
            pltpu.VMEM((rows, samples), jnp.bfloat16),
            pltpu.VMEM((windows, samples, width), jnp.bfloat16),
            pltpu.VMEM((blocks, cores, 2 * windows, NFREQ, width), jnp.bfloat16),
            pltpu.VMEM((lag_rows * width, depth), jnp.bfloat16),
            pltpu.SemaphoreType.DMA((windows,)),
            plain, plain, plain, plain, per_piece, plain, plain,
        ],
        compiler_params=pltpu.CompilerParams(
            collective_id=0, has_side_effects=True, vmem_limit_bytes=52 * 1024 * 1024
        ),
    )(plan, flags.reshape(1, width), jnp.swapaxes(record, 1, 2))


def solution(mesh):
    blocks, cores = mesh.shape["chan"], mesh.shape["tm"]
    small = cores == 2 and blocks == 4 * SPLIT
    return jax.shard_map(
        on_device_kernel if small else on_device_hops,
        mesh=mesh,
        in_specs=(P("tm", ("groups", "chan"), None), P(("groups", "chan")), P()),
        out_specs=P("tm", None, ("groups", "chan"), None),
        check_vma=False,
    )
```
